512 devices in a mesh: tm: 8 (over z), rows: 64 (over x, y, core).
Axes of the slice: x: 4, y: 8, z: 8, core: 2. Of those that a mesh axis runs over, the one named last changes fastest.
Arguments:
- features: bfloat16 [32, 96, 128, 256], P('tm', None, 'rows'), may hold values from -6 to 6
- gain_first: float32 [96], replicated, may hold values from 0.1 to 1.9
- conv_first: bfloat16 [3, 3, 3, 96, 96], replicated, may hold values from -0.125 to 0.125
- gain_second: float32 [96], replicated, may hold values from 0.1 to 1.9
- conv_second: bfloat16 [3, 3, 3, 96, 96], replicated, may hold values from -0.125 to 0.125
Outputs:
- decoded: bfloat16 [32, 96, 128, 256], P('tm', None, 'rows')
The draws below stay inside these ranges and needn't reach their ends.
All inputs are finite; a program needn't handle non-finite values.
Results may differ from the reference program's by a relative error of at most 0.004.
Values may be sent and summed in bfloat16 or wider, within the bound.
A program may use at most 64 MiB of HBM per device.

```python
import jax
import jax.numpy as jnp
from jax import lax

C = 96
W = 256
FRAMES = 32
HEIGHT = 128


def levels(key, extent, cuts, smallest, high):
    level = 1.0
    for dim, blocks in cuts:
        steps = jax.random.uniform(jax.random.fold_in(jax.random.fold_in(key, 6), dim), (blocks,), jnp.float32, smallest / len(cuts), high / len(cuts))
        level = level * jnp.repeat(jnp.exp(steps), extent[dim] // blocks).reshape((-1,) + (1,) * (len(extent) - 1 - dim))
    return level


def centred(key, extent, spread, reach, cuts=(), held_as=jnp.bfloat16):
    loudness = levels(key, extent, cuts, -0.22, 0.18) if cuts else 1.0
    entries = jax.random.normal(key, extent, jnp.float32) * spread * loudness
    return jnp.minimum(jnp.maximum(entries, -reach), reach).astype(held_as)


def setup_inputs(seed: int = 0) -> dict:
    key_list = jax.random.split(jax.random.key(seed), 6)
    features = centred(key_list[0], (FRAMES, C, HEIGHT, W), 1.0, 6.0, ((0, 8), (2, 64)))
    gain_first = jnp.clip(1.0 + 0.18 * jax.random.normal(key_list[1], (C,), jnp.float32), 0.1, 1.9)
    conv_first = centred(key_list[2], (3, 3, 3, C, C), (27 * C) ** -0.5, 0.125)
    gain_second = jnp.clip(1.0 + 0.18 * jax.random.normal(key_list[3], (C,), jnp.float32), 0.1, 1.9)
    conv_second = centred(key_list[4], (3, 3, 3, C, C), (27 * C) ** -0.5, 0.125)
    return {"features": features, "gain_first": gain_first, "conv_first": conv_first, "gain_second": gain_second, "conv_second": conv_second}


epsilon = 1e-06

def channel_norm(values, gain):
    mean_square = lax.optimization_barrier(jnp.mean(values * values, axis=1, keepdims=True))
    return values * lax.rsqrt(mean_square + epsilon) * gain[None, :, None, None]

def causal_conv(values, kernel):
    batched = jnp.transpose(values.astype(jnp.float32), (1, 0, 2, 3))[None]
    result = lax.conv_general_dilated(batched, kernel.astype(jnp.float32), window_strides=(1, 1, 1), padding=((2, 0), (1, 1), (1, 1)), dimension_numbers=('NCDHW', 'DHWOI', 'NCDHW'), precision=lax.Precision.HIGHEST)
    return jnp.transpose(result[0], (1, 0, 2, 3))

def reference(features, gain_first, conv_first, gain_second, conv_second):
    first = jax.nn.silu(channel_norm(features.astype(jnp.float32), gain_first)).astype(jnp.bfloat16)
    hidden = causal_conv(first, conv_first)
    second = jax.nn.silu(channel_norm(hidden, gain_second)).astype(jnp.bfloat16)
    mixed = causal_conv(second, conv_second)
    return (mixed + features.astype(jnp.float32)).astype(jnp.bfloat16)
```

```python
import functools

import jax
import jax.numpy as jnp
from jax import lax
from jax.experimental import pallas as pl
from jax.experimental.pallas import tpu as pltpu
from jax.sharding import PartitionSpec as P

MESH = pl.DeviceIdType.MESH
epsilon = 1e-06


def norm_silu(values, gain):
    mean_square = jnp.mean(values * values, axis=0, keepdims=True)
    v = values * lax.rsqrt(mean_square + epsilon) * gain
    return (v / (1.0 + jnp.exp(-v))).astype(jnp.bfloat16)


def stack_taps(taps, stacked):
    chan = taps.shape[-1]
    for e in range(3):
        stacked[chan * e : chan * (e + 1), :] = jnp.concatenate(
            [taps[a, b, e] for a in range(3) for b in range(3)], axis=1
        )


def as_column(row):
    chan = row.shape[0]
    wide = jnp.broadcast_to(row[None, :], (chan, chan))
    i = lax.broadcasted_iota(jnp.int32, (chan, chan), 0)
    j = lax.broadcasted_iota(jnp.int32, (chan, chan), 1)
    return jnp.sum(jnp.where(i == j, wide, 0.0), axis=1, keepdims=True)


def conv_row(cells, stacked, frame, row):
    chan, width = cells.shape[2], cells.shape[3]
    window = jnp.concatenate(
        [
            cells[frame - 2 + a, pl.ds(row, 3)].reshape(3 * chan, width)
            for a in range(3)
        ],
        axis=0,
    )
    p = jnp.dot(stacked[...], window, preferred_element_type=jnp.float32)
    column = lax.broadcasted_iota(jnp.int32, (chan, width), 1)
    before = jnp.where(column == 0, 0.0, pltpu.roll(p[:chan], 1, 1))
    after = jnp.where(
        column == width - 1, 0.0, pltpu.roll(p[2 * chan :], width - 1, 1)
    )
    return before + p[chan : 2 * chan] + after


def kernel(
    tm, rows, feat_hbm, gain1_hbm, taps1_hbm, gain2_hbm, taps2_hbm, out_hbm,
    feat, gain1, gain2, taps1, taps2, stack1, stack2, ext1, ext2, out,
    load_sem, store_sem, send_sem, recv_sem,
):
    t = lax.axis_index("tm")
    r = lax.axis_index("rows")
    core = lax.rem(r, 2)
    chan, width = feat.shape[1], feat.shape[3]
    last = feat.shape[0] + 2

    outer_at = r - 1 + 2 * core
    has_outer = jnp.logical_and(outer_at >= 0, outer_at < rows)
    outer = (t, jnp.clip(outer_at, 0, rows - 1))
    inner = (t, r + 1 - 2 * core)
    has_next = t < tm - 1
    has_prev = t > 0
    after = (jnp.minimum(t + 1, tm - 1), r)
    before = (jnp.maximum(t - 1, 0), r)
    own_outer, own_inner = 1 + core, 2 - core
    to_outer, to_inner = 3 - 3 * core, 3 * core

    barrier = pltpu.get_barrier_semaphore()
    pl.semaphore_signal(barrier, inc=1, device_id=inner, device_id_type=MESH)

    @pl.when(has_outer)
    def _():
        pl.semaphore_signal(barrier, inc=1, device_id=outer, device_id_type=MESH)

    @pl.when(has_prev)
    def _():
        pl.semaphore_signal(barrier, inc=1, device_id=before, device_id_type=MESH)

    order = (3, 2, 1, 0)
    feat_in = {
        f: pltpu.make_async_copy(feat_hbm.at[f], feat.at[f], load_sem.at[f])
        for f in order
    }
    rest_in = [
        pltpu.make_async_copy(src, dst, load_sem.at[4 + i])
        for i, (src, dst) in enumerate(
            ((gain1_hbm, gain1), (gain2_hbm, gain2), (taps1_hbm, taps1), (taps2_hbm, taps2))
        )
    ]
    rest_in[0].start()
    for f in order:
        feat_in[f].start()
    for copy in rest_in[1:]:
        copy.start()

    def remote(ext, n, src_frames, src_row, dst_frames, dst_row, device):
        return pltpu.make_async_remote_copy(
            src_ref=ext.at[src_frames, src_row],
            dst_ref=ext.at[dst_frames, dst_row],
            send_sem=send_sem.at[n],
            recv_sem=recv_sem.at[n],
            device_id=device,
            device_id_type=MESH,
        )

    def transfers(ext, n, cut):
        late, early = slice(cut, last), slice(2, cut)
        tail, head = slice(last - 2, last), slice(0, 2)
        return dict(
            z_outer=remote(ext, n, tail, own_outer, head, own_outer, after),
            z_inner=remote(ext, n + 1, tail, own_inner, head, own_inner, after),
            outer_late=remote(ext, n + 2, late, own_outer, late, to_outer, outer),
            outer_early=remote(ext, n + 3, early, own_outer, early, to_outer, outer),
            inner_late=remote(ext, n + 4, late, own_inner, late, to_inner, inner),
            inner_early=remote(ext, n + 5, early, own_inner, early, to_inner, inner),
            relay_outer=remote(ext, n + 6, head, own_outer, head, to_outer, outer),
            relay_inner=remote(ext, n + 7, head, own_inner, head, to_inner, inner),
        )

    moves1 = transfers(ext1, 0, 3)
    moves2 = transfers(ext2, 8, 4)
    both = jnp.logical_and(has_prev, has_outer)
    sends_if = dict(
        z_outer=has_next, z_inner=has_next, outer_late=has_outer, outer_early=has_outer,
        inner_late=None, inner_early=None, relay_outer=both, relay_inner=has_prev,
    )
    gets_if = dict(sends_if, z_outer=has_prev, z_inner=has_prev)

    def when(condition, action):
        if condition is None:
            action()
        else:
            pl.when(condition)(action)

    def send(moves, *names):
        for name in names:
            when(sends_if[name], moves[name].start)

    def got(moves, *names):
        for name in names:
            when(gets_if[name], moves[name].wait_recv)

    zero_row = jnp.zeros((chan, width), jnp.bfloat16)

    @pl.when(t == 0)
    def _():
        for ext in (ext1, ext2):
            for f in range(2):
                for row in range(4):
                    ext[f, row] = zero_row

    @pl.when(jnp.logical_not(has_outer))
    def _():
        for ext in (ext1, ext2):
            for f in range(last):
                ext[f, 3 * core] = zero_row

    rest_in[0].wait()
    column1 = as_column(gain1[...])

    def first(f):
        feat_in[f].wait()
        x = feat[f].astype(jnp.float32).reshape(chan, 2 * width)
        for row in range(2):
            ext1[2 + f, 1 + row] = norm_silu(x[:, row * width : (row + 1) * width], column1)

    first(3)
    first(2)
    neighbours = 1 + has_outer.astype(jnp.int32) + has_next.astype(jnp.int32)
    pl.semaphore_wait(barrier, neighbours)
    send(moves1, "z_outer", "z_inner")
    first(1)
    send(moves1, "outer_late", "inner_late")
    first(0)
    send(moves1, "outer_early", "inner_early")

    for copy in rest_in[1:]:
        copy.wait()
    stack_taps(taps1, stack1)
    column2 = as_column(gain2[...])

    def hidden(frame, row):
        return norm_silu(conv_row(ext1, stack1, frame, row), column2)

    got(moves1, "inner_late", "inner_early")
    for frame in (5, 4):
        ext2[frame, own_inner] = hidden(frame, 1 - core)
    stack_taps(taps2, stack2)
    got(moves1, "outer_late", "outer_early")
    for frame in (5, 4):
        ext2[frame, own_outer] = hidden(frame, core)
    send(moves2, "z_outer", "z_inner", "outer_late", "inner_late")
    got(moves1, "z_outer")
    send(moves1, "relay_outer")
    got(moves1, "z_inner")
    send(moves1, "relay_inner")
    got(moves1, "relay_outer", "relay_inner")
    for frame in (3, 2):
        for row in range(2):
            ext2[frame, 1 + row] = hidden(frame, row)
    send(moves2, "outer_early", "inner_early")

    def decoded(frame):
        mixed = jnp.concatenate(
            [conv_row(ext2, stack2, frame, row) for row in range(2)], axis=1
        )
        x = feat[frame - 2].astype(jnp.float32).reshape(chan, 2 * width)
        out[frame - 2] = (mixed + x).reshape(chan, 2, width).astype(jnp.bfloat16)
        copy = pltpu.make_async_copy(
            out.at[frame - 2], out_hbm.at[frame - 2], store_sem.at[frame - 2]
        )
        copy.start()
        return copy

    got(moves2, "z_outer")
    send(moves2, "relay_outer")
    got(moves2, "outer_late", "inner_late", "outer_early", "inner_early")
    stores = [decoded(5), decoded(4)]
    got(moves2, "z_inner")
    send(moves2, "relay_inner")
    got(moves2, "relay_outer", "relay_inner")
    stores += [decoded(3), decoded(2)]

    for moves in (moves1, moves2):
        for name, move in moves.items():
            when(sends_if[name], move.wait_send)
    for copy in stores:
        copy.wait()


def on_device(tm, rows, features, gain_first, conv_first, gain_second, conv_second):
    frames, chan, height, width = features.shape
    ext = pltpu.VMEM((frames + 2, height + 2, chan, width), jnp.bfloat16)
    stack = pltpu.VMEM((3 * chan, 9 * chan), jnp.bfloat16)
    return pl.pallas_call(
        functools.partial(kernel, tm, rows),
        out_shape=jax.ShapeDtypeStruct(features.shape, features.dtype),
        in_specs=[pl.BlockSpec(memory_space=pl.ANY)] * 5,
        out_specs=pl.BlockSpec(memory_space=pl.ANY),
        scratch_shapes=[
            pltpu.VMEM(features.shape, features.dtype),
            pltpu.VMEM(gain_first.shape, gain_first.dtype),
            pltpu.VMEM(gain_second.shape, gain_second.dtype),
            pltpu.VMEM(conv_first.shape, conv_first.dtype),
            pltpu.VMEM(conv_second.shape, conv_second.dtype),
            stack,
            stack,
            ext,
            ext,
            pltpu.VMEM(features.shape, features.dtype),
            pltpu.SemaphoreType.DMA((8,)),
            pltpu.SemaphoreType.DMA((4,)),
            pltpu.SemaphoreType.DMA((16,)),
            pltpu.SemaphoreType.DMA((16,)),
        ],
        compiler_params=pltpu.CompilerParams(
            collective_id=0, has_side_effects=True, vmem_limit_bytes=60 << 20
        ),
        cost_estimate=pl.CostEstimate(
            flops=4 * 27 * chan * chan * frames * height * width,
            bytes_accessed=3 << 20,
            transcendentals=0,
        ),
        name="residual_block",
    )(features, gain_first, conv_first, gain_second, conv_second)


def solution(mesh):
    placed = (P("tm", None, "rows", None), P(), P(), P(), P())
    return jax.shard_map(
        functools.partial(on_device, mesh.shape["tm"], mesh.shape["rows"]),
        mesh=mesh,
        in_specs=placed,
        out_specs=P("tm", None, "rows", None),
        check_vma=False,
    )
```

```python
import functools

import jax
import jax.numpy as jnp
from jax import lax
from jax.experimental import pallas as pl
from jax.experimental.pallas import tpu as pltpu
from jax.sharding import PartitionSpec as P

MESH = pl.DeviceIdType.MESH
epsilon = 1e-06


def norm_silu(values, gain):
    mean_square = jnp.mean(values * values, axis=0, keepdims=True)
    v = values * lax.rsqrt(mean_square + epsilon) * gain
    return (v / (1.0 + jnp.exp(-v))).astype(jnp.bfloat16)


def stack_taps(taps, own, edge):
    chan = taps.shape[-1]
    for row, (inside, beyond) in enumerate((((1, 2), 0), ((0, 1), 2))):
        for e in range(3):
            span = slice(chan * e, chan * (e + 1))
            own[row, span, :] = jnp.concatenate(
                [taps[a, b, e] for a in range(3) for b in inside], axis=1
            )
            edge[row, span, :] = jnp.concatenate(
                [taps[a, beyond, e] for a in range(3)], axis=1
            )


def as_column(row):
    chan = row.shape[0]
    wide = jnp.broadcast_to(row[None, :], (chan, chan))
    i = lax.broadcasted_iota(jnp.int32, (chan, chan), 0)
    j = lax.broadcasted_iota(jnp.int32, (chan, chan), 1)
    return jnp.sum(jnp.where(i == j, wide, 0.0), axis=1, keepdims=True)


def from_own(cells, stacked, frame, row):
    chan, width = cells.shape[2], cells.shape[3]
    window = [
        cells[frame - 2 + a, 1:3].reshape(2 * chan, width) for a in range(3)
    ]
    return jnp.dot(
        stacked[row], jnp.concatenate(window, axis=0), preferred_element_type=jnp.float32
    )


def from_edge(cells, stacked, frame, row):
    window = [cells[frame - 2 + a, 3 * row] for a in range(3)]
    return jnp.dot(
        stacked[row], jnp.concatenate(window, axis=0), preferred_element_type=jnp.float32
    )


def gather_columns(p):
    chan, width = p.shape[0] // 3, p.shape[1]
    column = lax.broadcasted_iota(jnp.int32, (chan, width), 1)
    before = jnp.where(column == 0, 0.0, pltpu.roll(p[:chan], 1, 1))
    after = jnp.where(
        column == width - 1, 0.0, pltpu.roll(p[2 * chan :], width - 1, 1)
    )
    return before + p[chan : 2 * chan] + after


def kernel(
    tm, rows, feat_hbm, gain1_hbm, taps1_hbm, gain2_hbm, taps2_hbm, out_hbm,
    feat, gain1, gain2, taps1, taps2, own1, edge1, own2, edge2, ext1, ext2, part, mixed, out,
    load_sem, store_sem, send_sem, recv_sem,
):
    t = lax.axis_index("tm")
    r = lax.axis_index("rows")
    core = lax.rem(r, 2)
    chan, width = feat.shape[1], feat.shape[3]
    last = feat.shape[0] + 2

    outer_at = r - 1 + 2 * core
    has_outer = jnp.logical_and(outer_at >= 0, outer_at < rows)
    outer = (t, jnp.clip(outer_at, 0, rows - 1))
    inner = (t, r + 1 - 2 * core)
    has_next = t < tm - 1
    has_prev = t > 0
    after = (jnp.minimum(t + 1, tm - 1), r)
    before = (jnp.maximum(t - 1, 0), r)
    own_outer, own_inner = 1 + core, 2 - core
    to_outer, to_inner = 3 - 3 * core, 3 * core

    barrier = pltpu.get_barrier_semaphore()
    pl.semaphore_signal(barrier, inc=1, device_id=inner, device_id_type=MESH)

    @pl.when(has_outer)
    def _():
        pl.semaphore_signal(barrier, inc=1, device_id=outer, device_id_type=MESH)

    @pl.when(has_prev)
    def _():
        pl.semaphore_signal(barrier, inc=1, device_id=before, device_id_type=MESH)

    order = (3, 2, 1, 0)
    feat_in = {
        f: pltpu.make_async_copy(feat_hbm.at[f], feat.at[f], load_sem.at[f])
        for f in order
    }
    rest_in = [
        pltpu.make_async_copy(src, dst, load_sem.at[4 + i])
        for i, (src, dst) in enumerate(
            ((gain1_hbm, gain1), (gain2_hbm, gain2), (taps1_hbm, taps1), (taps2_hbm, taps2))
        )
    ]
    rest_in[0].start()
    for f in order:
        feat_in[f].start()
    for copy in rest_in[1:]:
        copy.start()

    def remote(ext, n, src_frames, src_row, dst_frames, dst_row, device):
        return pltpu.make_async_remote_copy(
            src_ref=ext.at[src_frames, src_row],
            dst_ref=ext.at[dst_frames, dst_row],
            send_sem=send_sem.at[n],
            recv_sem=recv_sem.at[n],
            device_id=device,
            device_id_type=MESH,
        )

    both = jnp.logical_and(has_prev, has_outer)
    moves = {}

    def plan_z(name, ext, row, cuts):
        for i, (low, high) in enumerate(cuts):
            moves[name, i] = (
                remote(ext, len(moves), slice(low + 4, high + 4), row, slice(low, high), row, after),
                has_next,
                has_prev,
            )

    def plan_rows(name, ext, cuts, relayed=False):
        for i, (low, high) in enumerate(cuts):
            frames = slice(low, high)
            condition = both if relayed else has_outer
            moves[name + "_outer", i] = (
                remote(ext, len(moves), frames, own_outer, frames, to_outer, outer),
                condition,
                condition,
            )
            condition = has_prev if relayed else None
            moves[name + "_inner", i] = (
                remote(ext, len(moves), frames, own_inner, frames, to_inner, inner),
                condition,
                condition,
            )

    plan_z("z1_outer", ext1, own_outer, ((0, 1), (1, 2)))
    plan_z("z1_inner", ext1, own_inner, ((0, 2),))
    plan_rows("late1", ext1, ((3, 6),))
    plan_rows("early1", ext1, ((2, 3),))
    plan_rows("relay1", ext1, ((0, 1), (1, 2)), True)
    plan_z("z2_outer", ext2, own_outer, ((0, 1), (1, 2)))
    plan_z("z2_inner", ext2, own_inner, ((0, 2),))
    plan_rows("late2", ext2, ((4, 6),))
    plan_rows("early2", ext2, ((2, 4),))
    plan_rows("relay2", ext2, ((0, 1), (1, 2)), True)

    def when(condition, action):
        if condition is None:
            action()
        else:
            pl.when(condition)(action)

    def send(name, i=0):
        copy, sends, _ = moves[name, i]
        when(sends, copy.start)

    def got(name, i=0):
        copy, _, gets = moves[name, i]
        when(gets, copy.wait_recv)

    zero_row = jnp.zeros((chan, width), jnp.bfloat16)

    @pl.when(t == 0)
    def _():
        for ext in (ext1, ext2):
            for f in range(2):
                for row in range(4):
                    ext[f, row] = zero_row

    @pl.when(jnp.logical_not(has_outer))
    def _():
        for ext in (ext1, ext2):
            for f in range(last):
                ext[f, 3 * core] = zero_row

    rest_in[0].wait()
    column1 = as_column(gain1[...])

    def first(f):
        feat_in[f].wait()
        x = feat[f].astype(jnp.float32).reshape(chan, 2 * width)
        for row in range(2):
            ext1[2 + f, 1 + row] = norm_silu(x[:, row * width : (row + 1) * width], column1)

    first(3)
    first(2)
    neighbours = 1 + has_outer.astype(jnp.int32) + has_next.astype(jnp.int32)
    pl.semaphore_wait(barrier, neighbours)
    for i in (0, 1):
        send("z1_outer", i)
    first(1)
    send("late1_outer")
    send("late1_inner")
    first(0)
    send("early1_outer")
    send("early1_inner")

    out_outer, out_inner = core, 1 - core

    def start1(frame):
        for row in range(2):
            part[frame - 2, row] = from_own(ext1, own1, frame, row)

    def second(frame, row):
        p = part[frame - 2, row] + from_edge(ext1, edge1, frame, row)
        ext2[frame, 1 + row] = norm_silu(gather_columns(p), column2)

    for copy in rest_in[1:]:
        copy.wait()
    stack_taps(taps1, own1, edge1)
    column2 = as_column(gain2[...])
    start1(5)
    start1(4)
    send("z1_inner")
    got("late1_inner")
    got("early1_inner")
    second(5, out_inner)
    second(4, out_inner)
    stack_taps(taps2, own2, edge2)
    got("z1_outer", 0)
    send("relay1_outer", 0)
    got("late1_outer")
    second(5, out_outer)
    send("z2_outer", 1)
    got("z1_outer", 1)
    send("relay1_outer", 1)
    got("early1_outer")
    second(4, out_outer)
    send("z2_outer", 0)
    send("late2_outer")
    send("late2_inner")
    got("z1_inner")
    for i in range(2):
        send("relay1_inner", i)
    send("z2_inner")
    start1(3)
    start1(2)
    for i in range(2):
        got("relay1_outer", i)
    second(3, out_outer)
    second(2, out_outer)
    send("early2_outer")
    for i in range(2):
        got("relay1_inner", i)
    second(3, out_inner)
    second(2, out_inner)
    send("early2_inner")

    def start2(frame):
        for row in range(2):
            part[frame - 2, row] = from_own(ext2, own2, frame, row)

    def mix(frame, row):
        p = part[frame - 2, row] + from_edge(ext2, edge2, frame, row)
        mixed[frame - 2, row] = gather_columns(p)

    stores = []

    def finish(frame):
        x = feat[frame - 2].astype(jnp.float32).reshape(chan, 2 * width)
        total = jnp.concatenate([mixed[frame - 2, 0], mixed[frame - 2, 1]], axis=1) + x
        out[frame - 2] = total.reshape(chan, 2, width).astype(jnp.bfloat16)
        copy = pltpu.make_async_copy(
            out.at[frame - 2], out_hbm.at[frame - 2], store_sem.at[frame - 2]
        )
        copy.start()
        stores.append(copy)

    for i in (1, 0):
        got("z2_outer", i)
        send("relay2_outer", i)
    start2(5)
    start2(4)
    got("late2_inner")
    got("early2_inner")
    mix(5, out_inner)
    mix(4, out_inner)
    got("z2_inner")
    for i in range(2):
        send("relay2_inner", i)
    start2(3)
    start2(2)
    got("late2_outer")
    got("early2_outer")
    mix(5, out_outer)
    mix(4, out_outer)
    finish(5)
    finish(4)
    for i in range(2):
        got("relay2_outer", i)
    mix(3, out_outer)
    mix(2, out_outer)
    for i in range(2):
        got("relay2_inner", i)
    mix(3, out_inner)
    mix(2, out_inner)
    finish(3)
    finish(2)

    for copy, sends, _ in moves.values():
        when(sends, copy.wait_send)
    for copy in stores:
        copy.wait()


def on_device(tm, rows, features, gain_first, conv_first, gain_second, conv_second):
    frames, chan, height, width = features.shape
    ext = pltpu.VMEM((frames + 2, height + 2, chan, width), jnp.bfloat16)
    own = pltpu.VMEM((2, 3 * chan, 6 * chan), jnp.bfloat16)
    edge = pltpu.VMEM((2, 3 * chan, 3 * chan), jnp.bfloat16)
    return pl.pallas_call(
        functools.partial(kernel, tm, rows),
        out_shape=jax.ShapeDtypeStruct(features.shape, features.dtype),
        in_specs=[pl.BlockSpec(memory_space=pl.ANY)] * 5,
        out_specs=pl.BlockSpec(memory_space=pl.ANY),
        scratch_shapes=[
            pltpu.VMEM(features.shape, features.dtype),
            pltpu.VMEM(gain_first.shape, gain_first.dtype),
            pltpu.VMEM(gain_second.shape, gain_second.dtype),
            pltpu.VMEM(conv_first.shape, conv_first.dtype),
            pltpu.VMEM(conv_second.shape, conv_second.dtype),
            own,
            edge,
            own,
            edge,
            ext,
            ext,
            pltpu.VMEM((frames, height, 3 * chan, width), jnp.float32),
            pltpu.VMEM((frames, height, chan, width), jnp.float32),
            pltpu.VMEM(features.shape, features.dtype),
            pltpu.SemaphoreType.DMA((8,)),
            pltpu.SemaphoreType.DMA((4,)),
            pltpu.SemaphoreType.DMA((32,)),
            pltpu.SemaphoreType.DMA((32,)),
        ],
        compiler_params=pltpu.CompilerParams(
            collective_id=0, has_side_effects=True, vmem_limit_bytes=60 << 20
        ),
        cost_estimate=pl.CostEstimate(
            flops=4 * 27 * chan * chan * frames * height * width,
            bytes_accessed=3 << 20,
            transcendentals=0,
        ),
        name="residual_block",
    )(features, gain_first, conv_first, gain_second, conv_second)


def solution(mesh):
    placed = (P("tm", None, "rows", None), P(), P(), P(), P())
    return jax.shard_map(
        functools.partial(on_device, mesh.shape["tm"], mesh.shape["rows"]),
        mesh=mesh,
        in_specs=placed,
        out_specs=P("tm", None, "rows", None),
        check_vma=False,
    )
```

```python
import functools

import jax
import jax.numpy as jnp
from jax import lax
from jax.experimental import pallas as pl
from jax.experimental.pallas import tpu as pltpu
from jax.sharding import PartitionSpec as P

MESH = pl.DeviceIdType.MESH
epsilon = 1e-06


def norm_silu(values, gain):
    mean_square = jnp.mean(values * values, axis=0, keepdims=True)
    v = values * lax.rsqrt(mean_square + epsilon) * gain
    return (v / (1.0 + jnp.exp(-v))).astype(jnp.bfloat16)


def stack_taps(taps, own, edge):
    chan = taps.shape[-1]
    depth = own.shape[-1]
    for row, (inside, beyond) in enumerate((((1, 2), 0), ((0, 1), 2))):
        for e in range(3):
            span = slice(chan * e, chan * (e + 1))
            wide = jnp.concatenate(
                [taps[a, b, e] for a in range(3) for b in inside]
                + [taps[a, beyond, e] for a in range(3)],
                axis=1,
            )
            own[row, span, :] = wide[:, :depth]
            edge[row, span, :] = wide[:, depth:]


def as_column(row):
    chan = row.shape[0]
    wide = jnp.broadcast_to(row[None, :], (chan, chan))
    i = lax.broadcasted_iota(jnp.int32, (chan, chan), 0)
    j = lax.broadcasted_iota(jnp.int32, (chan, chan), 1)
    return jnp.sum(jnp.where(i == j, wide, 0.0), axis=1, keepdims=True)


def from_own(cells, stacked, frame, row):
    chan, width = cells.shape[2], cells.shape[3]
    window = [
        cells[frame - 2, 1:3].reshape(2 * chan, width),
        cells[frame - 1, 1:3].reshape(2 * chan, width),
        cells[frame, 1],
        cells[frame, 2, : stacked.shape[-1] - 5 * chan],
    ]
    return jnp.dot(
        stacked[row], jnp.concatenate(window, axis=0), preferred_element_type=jnp.float32
    )


def from_edge(cells, stacked, frame, row):
    chan = cells.shape[2]
    window = [cells[frame, 2, 4 * chan - stacked.shape[-1] :]]
    window += [cells[frame - 2 + a, 3 * row] for a in range(3)]
    return jnp.dot(
        stacked[row], jnp.concatenate(window, axis=0), preferred_element_type=jnp.float32
    )


def gather_columns(p):
    chan, width = p.shape[0] // 3, p.shape[1]
    column = lax.broadcasted_iota(jnp.int32, (chan, width), 1)
    before = jnp.where(column == 0, 0.0, pltpu.roll(p[:chan], 1, 1))
    after = jnp.where(
        column == width - 1, 0.0, pltpu.roll(p[2 * chan :], width - 1, 1)
    )
    return before + p[chan : 2 * chan] + after


def kernel(
    tm, rows, feat_hbm, gain1_hbm, taps1_hbm, gain2_hbm, taps2_hbm, out,
    feat, gain1, gain2, taps1, taps2, own1, edge1, own2, edge2, ext1, ext2, part, mixed,
    load_sem, send_sem, recv_sem,
):
    t = lax.axis_index("tm")
    r = lax.axis_index("rows")
    core = lax.rem(r, 2)
    chan, width = feat.shape[1], feat.shape[3]
    last = feat.shape[0] + 2

    outer_at = r - 1 + 2 * core
    has_outer = jnp.logical_and(outer_at >= 0, outer_at < rows)
    outer = (t, jnp.clip(outer_at, 0, rows - 1))
    inner = (t, r + 1 - 2 * core)
    has_next = t < tm - 1
    has_prev = t > 0
    after = (jnp.minimum(t + 1, tm - 1), r)
    before = (jnp.maximum(t - 1, 0), r)
    own_outer, own_inner = 1 + core, 2 - core
    to_outer, to_inner = 3 - 3 * core, 3 * core

    barrier = pltpu.get_barrier_semaphore()
    pl.semaphore_signal(barrier, inc=1, device_id=inner, device_id_type=MESH)

    @pl.when(has_outer)
    def _():
        pl.semaphore_signal(barrier, inc=1, device_id=outer, device_id_type=MESH)

    @pl.when(has_prev)
    def _():
        pl.semaphore_signal(barrier, inc=1, device_id=before, device_id_type=MESH)

    order = (3, 2, 1, 0)
    feat_in = {
        f: pltpu.make_async_copy(feat_hbm.at[f], feat.at[f], load_sem.at[f])
        for f in order
    }
    rest_in = [
        pltpu.make_async_copy(src, dst, load_sem.at[4 + i])
        for i, (src, dst) in enumerate(
            ((gain1_hbm, gain1), (gain2_hbm, gain2), (taps1_hbm, taps1), (taps2_hbm, taps2))
        )
    ]
    rest_in[0].start()
    for f in order:
        feat_in[f].start()
    for copy in rest_in[1:]:
        copy.start()

    def remote(ext, n, src_frames, src_row, dst_frames, dst_row, device):
        return pltpu.make_async_remote_copy(
            src_ref=ext.at[src_frames, src_row],
            dst_ref=ext.at[dst_frames, dst_row],
            send_sem=send_sem.at[n],
            recv_sem=recv_sem.at[n],
            device_id=device,
            device_id_type=MESH,
        )

    both = jnp.logical_and(has_prev, has_outer)
    moves = {}

    def plan_z(name, ext, row, cuts):
        for i, (low, high) in enumerate(cuts):
            moves[name, i] = (
                remote(ext, len(moves), slice(low + 4, high + 4), row, slice(low, high), row, after),
                has_next,
                has_prev,
            )

    def plan_rows(name, ext, cuts, relayed=False):
        for i, (low, high) in enumerate(cuts):
            frames = slice(low, high)
            condition = both if relayed else has_outer
            moves[name + "_outer", i] = (
                remote(ext, len(moves), frames, own_outer, frames, to_outer, outer),
                condition,
                condition,
            )
            condition = has_prev if relayed else None
            moves[name + "_inner", i] = (
                remote(ext, len(moves), frames, own_inner, frames, to_inner, inner),
                condition,
                condition,
            )

    plan_z("z1_outer", ext1, own_outer, ((0, 1), (1, 2)))
    plan_z("z1_inner", ext1, own_inner, ((0, 2),))
    plan_rows("late1", ext1, ((3, 6),))
    plan_rows("early1", ext1, ((2, 3),))
    plan_rows("relay1", ext1, ((0, 1), (1, 2)), True)
    plan_z("z2_outer", ext2, own_outer, ((0, 1), (1, 2)))
    plan_z("z2_inner", ext2, own_inner, ((0, 2),))
    plan_rows("late2", ext2, ((4, 6),))
    plan_rows("early2", ext2, ((2, 4),))
    plan_rows("relay2", ext2, ((0, 1), (1, 2)), True)

    def when(condition, action):
        if condition is None:
            action()
        else:
            pl.when(condition)(action)

    def send(name, i=0):
        copy, sends, _ = moves[name, i]
        when(sends, copy.start)

    def got(name, i=0):
        copy, _, gets = moves[name, i]
        when(gets, copy.wait_recv)

    zero_row = jnp.zeros((chan, width), jnp.bfloat16)

    @pl.when(t == 0)
    def _():
        for ext in (ext1, ext2):
            for f in range(2):
                for row in range(4):
                    ext[f, row] = zero_row

    @pl.when(jnp.logical_not(has_outer))
    def _():
        for ext in (ext1, ext2):
            for f in range(last):
                ext[f, 3 * core] = zero_row

    rest_in[0].wait()
    column1 = as_column(gain1[...])

    def first(f):
        feat_in[f].wait()
        x = feat[f].astype(jnp.float32).reshape(chan, 2 * width)
        for row in range(2):
            ext1[2 + f, 1 + row] = norm_silu(x[:, row * width : (row + 1) * width], column1)

    first(3)
    first(2)
    neighbours = 1 + has_outer.astype(jnp.int32) + has_next.astype(jnp.int32)
    pl.semaphore_wait(barrier, neighbours)
    for i in (1, 0):
        send("z1_outer", i)
    first(1)
    send("late1_outer")
    send("late1_inner")
    first(0)
    send("early1_outer")
    send("early1_inner")

    out_outer, out_inner = core, 1 - core

    def start1(frame):
        for row in range(2):
            part[frame - 2, row] = from_own(ext1, own1, frame, row)

    def second(frame, row):
        p = part[frame - 2, row] + from_edge(ext1, edge1, frame, row)
        ext2[frame, 1 + row] = norm_silu(gather_columns(p), column2)

    for copy in rest_in[1:]:
        copy.wait()
    stack_taps(taps1, own1, edge1)
    column2 = as_column(gain2[...])
    start1(5)
    start1(4)
    send("z1_inner")
    got("late1_inner")
    got("early1_inner")
    second(5, out_inner)
    second(4, out_inner)
    stack_taps(taps2, own2, edge2)
    got("z1_outer", 0)
    send("relay1_outer", 0)
    got("late1_outer")
    second(5, out_outer)
    send("z2_outer", 1)
    got("z1_outer", 1)
    send("relay1_outer", 1)
    got("early1_outer")
    second(4, out_outer)
    send("z2_outer", 0)
    send("late2_outer")
    send("late2_inner")
    got("z1_inner")
    for i in range(2):
        send("relay1_inner", i)
    send("z2_inner")
    start1(3)
    start1(2)
    for i in range(2):
        got("relay1_outer", i)
    second(3, out_outer)
    second(2, out_outer)
    send("early2_outer")
    for i in range(2):
        got("relay1_inner", i)
    second(3, out_inner)
    second(2, out_inner)
    send("early2_inner")

    def start2(frame):
        for row in range(2):
            part[frame - 2, row] = from_own(ext2, own2, frame, row)

    def mix(frame, row):
        p = part[frame - 2, row] + from_edge(ext2, edge2, frame, row)
        mixed[frame - 2, row] = gather_columns(p)

    def finish(frame):
        x = feat[frame - 2].astype(jnp.float32).reshape(chan, 2 * width)
        total = jnp.concatenate([mixed[frame - 2, 0], mixed[frame - 2, 1]], axis=1) + x
        out[frame - 2] = total.reshape(chan, 2, width).astype(jnp.bfloat16)

    for i in (1, 0):
        got("z2_outer", i)
        send("relay2_outer", i)
    start2(5)
    start2(4)
    got("late2_inner")
    got("early2_inner")
    mix(5, out_inner)
    mix(4, out_inner)
    got("z2_inner")
    for i in range(2):
        send("relay2_inner", i)
    start2(3)
    start2(2)
    got("late2_outer")
    got("early2_outer")
    mix(5, out_outer)
    mix(4, out_outer)
    finish(5)
    finish(4)
    for i in range(2):
        got("relay2_outer", i)
    mix(3, out_outer)
    mix(2, out_outer)
    for i in range(2):
        got("relay2_inner", i)
    mix(3, out_inner)
    finish(3)
    mix(2, out_inner)
    finish(2)

    for copy, sends, _ in moves.values():
        when(sends, copy.wait_send)


def on_device(tm, rows, features, gain_first, conv_first, gain_second, conv_second):
    frames, chan, height, width = features.shape
    ext = pltpu.VMEM((frames + 2, height + 2, chan, width), jnp.bfloat16)
    depth = 6 * chan // 256 * 256
    own = pltpu.VMEM((2, 3 * chan, depth), jnp.bfloat16)
    edge = pltpu.VMEM((2, 3 * chan, 9 * chan - depth), jnp.bfloat16)
    operands = (features, gain_first, conv_first, gain_second, conv_second)
    operands = [pltpu.with_memory_space_constraint(x, pltpu.HBM) for x in operands]
    return pl.pallas_call(
        functools.partial(kernel, tm, rows),
        out_shape=pltpu.VMEM(features.shape, features.dtype),
        in_specs=[pl.BlockSpec(memory_space=pl.ANY)] * 5,
        out_specs=pl.BlockSpec(memory_space=pltpu.VMEM),
        scratch_shapes=[
            pltpu.VMEM(features.shape, features.dtype),
            pltpu.VMEM(gain_first.shape, gain_first.dtype),
            pltpu.VMEM(gain_second.shape, gain_second.dtype),
            pltpu.VMEM(conv_first.shape, conv_first.dtype),
            pltpu.VMEM(conv_second.shape, conv_second.dtype),
            own,
            edge,
            own,
            edge,
            ext,
            ext,
            pltpu.VMEM((frames, height, 3 * chan, width), jnp.float32),
            pltpu.VMEM((frames, height, chan, width), jnp.float32),
            pltpu.SemaphoreType.DMA((8,)),
            pltpu.SemaphoreType.DMA((40,)),
            pltpu.SemaphoreType.DMA((40,)),
        ],
        compiler_params=pltpu.CompilerParams(
            collective_id=0, has_side_effects=True, vmem_limit_bytes=32 << 20
        ),
        cost_estimate=pl.CostEstimate(
            flops=4 * 27 * chan * chan * frames * height * width,
            bytes_accessed=3 << 20,
            transcendentals=0,
        ),
        name="residual_block",
    )(*operands)


def solution(mesh):
    placed = (P("tm", None, "rows", None), P(), P(), P(), P())
    return jax.shard_map(
        functools.partial(on_device, mesh.shape["tm"], mesh.shape["rows"]),
        mesh=mesh,
        in_specs=placed,
        out_specs=P("tm", None, "rows", None),
        check_vma=False,
    )
```

```python
import functools

import jax
import jax.numpy as jnp
from jax import lax
from jax.experimental import pallas as pl
from jax.experimental.pallas import tpu as pltpu
from jax.sharding import PartitionSpec as P

MESH = pl.DeviceIdType.MESH
epsilon = 1e-06


def norm_silu(values, gain):
    mean_square = jnp.mean(values * values, axis=0, keepdims=True)
    v = values * lax.rsqrt(mean_square + epsilon) * gain
    return (v / (1.0 + jnp.exp(-v))).astype(jnp.bfloat16)


def stack_taps(taps, own, edge):
    chan = taps.shape[-1]
    depth = own.shape[-1]
    for row, (inside, beyond) in enumerate((((1, 2), 0), ((0, 1), 2))):
        for e in range(3):
            span = slice(chan * e, chan * (e + 1))
            wide = jnp.concatenate(
                [taps[a, b, e] for a in range(3) for b in inside]
                + [taps[a, beyond, e] for a in range(3)],
                axis=1,
            )
            own[row, span, :] = wide[:, :depth]
            edge[row, span, :] = wide[:, depth:]


def as_column(row):
    chan = row.shape[0]
    wide = jnp.broadcast_to(row[None, :], (chan, chan))
    i = lax.broadcasted_iota(jnp.int32, (chan, chan), 0)
    j = lax.broadcasted_iota(jnp.int32, (chan, chan), 1)
    return jnp.sum(jnp.where(i == j, wide, 0.0), axis=1, keepdims=True)


def from_own(cells, stacked, frame, row):
    chan, width = cells.shape[2], cells.shape[3]
    window = [
        cells[frame - 2, 1:3].reshape(2 * chan, width),
        cells[frame - 1, 1:3].reshape(2 * chan, width),
        cells[frame, 1],
        cells[frame, 2, : stacked.shape[-1] - 5 * chan],
    ]
    return jnp.dot(
        stacked[row], jnp.concatenate(window, axis=0), preferred_element_type=jnp.float32
    )


def from_edge(cells, stacked, frame, row):
    chan = cells.shape[2]
    window = [cells[frame, 2, 4 * chan - stacked.shape[-1] :]]
    window += [cells[frame - 2 + a, 3 * row] for a in range(3)]
    return jnp.dot(
        stacked[row], jnp.concatenate(window, axis=0), preferred_element_type=jnp.float32
    )


def gather_columns(p):
    chan, width = p.shape[0] // 3, p.shape[1]
    column = lax.broadcasted_iota(jnp.int32, (chan, width), 1)
    before = jnp.where(column == 0, 0.0, pltpu.roll(p[:chan], 1, 1))
    after = jnp.where(
        column == width - 1, 0.0, pltpu.roll(p[2 * chan :], width - 1, 1)
    )
    return before + p[chan : 2 * chan] + after


def kernel(
    tm, rows, feat_hbm, gain1_hbm, taps1_hbm, gain2_hbm, taps2_hbm, out,
    feat, gain1, gain2, taps1, taps2, own1, edge1, own2, edge2, ext1, ext2, part, mixed,
    load_sem, send_sem, recv_sem,
):
    t = lax.axis_index("tm")
    r = lax.axis_index("rows")
    core = lax.rem(r, 2)
    chan, width = feat.shape[1], feat.shape[3]
    last = feat.shape[0] + 2

    outer_at = r - 1 + 2 * core
    has_outer = jnp.logical_and(outer_at >= 0, outer_at < rows)
    outer = (t, jnp.clip(outer_at, 0, rows - 1))
    inner = (t, r + 1 - 2 * core)
    has_next = t < tm - 1
    has_prev = t > 0
    after = (jnp.minimum(t + 1, tm - 1), r)
    before = (jnp.maximum(t - 1, 0), r)
    own_outer, own_inner = 1 + core, 2 - core
    to_outer, to_inner = 3 - 3 * core, 3 * core

    barrier = pltpu.get_barrier_semaphore()
    pl.semaphore_signal(barrier, inc=1, device_id=inner, device_id_type=MESH)

    @pl.when(has_outer)
    def _():
        pl.semaphore_signal(barrier, inc=1, device_id=outer, device_id_type=MESH)

    @pl.when(has_prev)
    def _():
        pl.semaphore_signal(barrier, inc=1, device_id=before, device_id_type=MESH)

    order = (3, 2, 1, 0)
    feat_in = {
        f: pltpu.make_async_copy(feat_hbm.at[f], feat.at[f], load_sem.at[f])
        for f in order
    }
    rest_in = [
        pltpu.make_async_copy(src, dst, load_sem.at[4 + i])
        for i, (src, dst) in enumerate(
            ((gain1_hbm, gain1), (gain2_hbm, gain2), (taps1_hbm, taps1), (taps2_hbm, taps2))
        )
    ]
    rest_in[0].start()
    for f in order:
        feat_in[f].start()
    for copy in rest_in[1:]:
        copy.start()

    def remote(ext, n, src_frames, src_row, dst_frames, dst_row, device):
        return pltpu.make_async_remote_copy(
            src_ref=ext.at[src_frames, src_row],
            dst_ref=ext.at[dst_frames, dst_row],
            send_sem=send_sem.at[n],
            recv_sem=recv_sem.at[n],
            device_id=device,
            device_id_type=MESH,
        )

    both = jnp.logical_and(has_prev, has_outer)
    moves = {}

    def plan_z(name, ext, row, cuts):
        for i, (low, high) in enumerate(cuts):
            moves[name, i] = (
                remote(ext, len(moves), slice(low + 4, high + 4), row, slice(low, high), row, after),
                has_next,
                has_prev,
            )

    def plan_rows(name, ext, cuts, relayed=False):
        for i, (low, high) in enumerate(cuts):
            frames = slice(low, high)
            condition = both if relayed else has_outer
            moves[name + "_outer", i] = (
                remote(ext, len(moves), frames, own_outer, frames, to_outer, outer),
                condition,
                condition,
            )
            condition = has_prev if relayed else None
            moves[name + "_inner", i] = (
                remote(ext, len(moves), frames, own_inner, frames, to_inner, inner),
                condition,
                condition,
            )

    halves = ((0, 1), (1, 2))
    plan_z("z1_outer", ext1, own_outer, halves)
    plan_z("z1_inner", ext1, own_inner, ((0, 2),))
    plan_rows("rows1", ext1, ((2, 3), (3, 4), (4, 5), (5, 6)))
    plan_rows("relay1", ext1, halves, True)
    plan_z("z2_outer", ext2, own_outer, halves)
    plan_z("z2_inner", ext2, own_inner, halves)
    plan_rows("late2", ext2, ((4, 6),))
    plan_rows("early2", ext2, ((2, 3), (3, 4)))
    plan_rows("relay2", ext2, halves, True)

    def when(condition, action):
        if condition is None:
            action()
        else:
            pl.when(condition)(action)

    def send(name, i=0):
        copy, sends, _ = moves[name, i]
        when(sends, copy.start)

    def got(name, i=0):
        copy, _, gets = moves[name, i]
        when(gets, copy.wait_recv)

    zero_row = jnp.zeros((chan, width), jnp.bfloat16)

    @pl.when(t == 0)
    def _():
        for ext in (ext1, ext2):
            for f in range(2):
                for row in range(4):
                    ext[f, row] = zero_row

    @pl.when(jnp.logical_not(has_outer))
    def _():
        for ext in (ext1, ext2):
            for f in range(last):
                ext[f, 3 * core] = zero_row

    rest_in[0].wait()
    column1 = as_column(gain1[...])

    def first(f):
        feat_in[f].wait()
        x = feat[f].astype(jnp.float32).reshape(chan, 2 * width)
        for row in range(2):
            ext1[2 + f, 1 + row] = norm_silu(x[:, row * width : (row + 1) * width], column1)

    neighbours = 1 + has_outer.astype(jnp.int32) + has_next.astype(jnp.int32)
    for f in order:
        first(f)
        if f == 3:
            pl.semaphore_wait(barrier, neighbours)
            send("z1_outer", 1)
        send("rows1_outer", f)
        send("rows1_inner", f)
    send("z1_outer", 0)

    out_outer, out_inner = core, 1 - core

    def start1(frame):
        for row in range(2):
            part[frame - 2, row] = from_own(ext1, own1, frame, row)

    def second(frame, row):
        p = part[frame - 2, row] + from_edge(ext1, edge1, frame, row)
        ext2[frame, 1 + row] = norm_silu(gather_columns(p), column2)

    for copy in rest_in[1:]:
        copy.wait()
    stack_taps(taps1, own1, edge1)
    column2 = as_column(gain2[...])
    start1(5)
    start1(4)
    for f in order:
        got("rows1_inner", f)
    send("z1_inner")
    second(5, out_inner)
    second(4, out_inner)
    stack_taps(taps2, own2, edge2)
    got("z1_outer", 1)
    send("relay1_outer", 1)
    send("z2_inner", 1)
    for f in order[:3]:
        got("rows1_outer", f)
    second(5, out_outer)
    send("z2_outer", 1)
    got("z1_outer", 0)
    send("relay1_outer", 0)
    got("rows1_outer", 0)
    second(4, out_outer)
    send("z2_outer", 0)
    send("late2_outer")
    send("late2_inner")
    got("z1_inner")
    for i in (1, 0):
        send("relay1_inner", i)
    send("z2_inner", 0)
    start1(3)
    start1(2)
    got("relay1_outer", 1)
    second(3, out_outer)
    send("early2_outer", 1)
    got("relay1_outer", 0)
    second(2, out_outer)
    send("early2_outer", 0)
    got("z2_inner", 1)
    send("relay2_inner", 1)
    for i in (1, 0):
        got("relay1_inner", i)
    second(3, out_inner)
    second(2, out_inner)
    for i in (1, 0):
        send("early2_inner", i)
    got("z2_outer", 1)
    send("relay2_outer", 1)

    def start2(frame):
        for row in range(2):
            part[frame - 2, row] = from_own(ext2, own2, frame, row)

    def mix(frame, row):
        p = part[frame - 2, row] + from_edge(ext2, edge2, frame, row)
        mixed[frame - 2, row] = gather_columns(p)

    def finish(frame):
        x = feat[frame - 2].astype(jnp.float32).reshape(chan, 2 * width)
        total = jnp.concatenate([mixed[frame - 2, 0], mixed[frame - 2, 1]], axis=1) + x
        out[frame - 2] = total.reshape(chan, 2, width).astype(jnp.bfloat16)

    start2(5)
    start2(4)
    got("z2_outer", 0)
    send("relay2_outer", 0)
    got("late2_inner")
    for i in (1, 0):
        got("early2_inner", i)
    mix(5, out_inner)
    mix(4, out_inner)
    start2(3)
    got("z2_inner", 0)
    send("relay2_inner", 0)
    start2(2)
    got("late2_outer")
    for i in (1, 0):
        got("early2_outer", i)
    mix(5, out_outer)
    mix(4, out_outer)
    finish(5)
    finish(4)
    got("relay2_outer", 1)
    got("relay2_inner", 1)
    mix(3, 0)
    mix(3, 1)
    finish(3)
    got("relay2_outer", 0)
    got("relay2_inner", 0)
    mix(2, 0)
    mix(2, 1)
    finish(2)

    for copy, sends, _ in moves.values():
        when(sends, copy.wait_send)


def on_device(tm, rows, features, gain_first, conv_first, gain_second, conv_second):
    frames, chan, height, width = features.shape
    ext = pltpu.VMEM((frames + 2, height + 2, chan, width), jnp.bfloat16)
    depth = 6 * chan // 256 * 256
    own = pltpu.VMEM((2, 3 * chan, depth), jnp.bfloat16)
    edge = pltpu.VMEM((2, 3 * chan, 9 * chan - depth), jnp.bfloat16)
    operands = (features, gain_first, conv_first, gain_second, conv_second)
    operands = [pltpu.with_memory_space_constraint(x, pltpu.HBM) for x in operands]
    return pl.pallas_call(
        functools.partial(kernel, tm, rows),
        out_shape=pltpu.VMEM(features.shape, features.dtype),
        in_specs=[pl.BlockSpec(memory_space=pl.ANY)] * 5,
        out_specs=pl.BlockSpec(memory_space=pltpu.VMEM),
        scratch_shapes=[
            pltpu.VMEM(features.shape, features.dtype),
            pltpu.VMEM(gain_first.shape, gain_first.dtype),
            pltpu.VMEM(gain_second.shape, gain_second.dtype),
            pltpu.VMEM(conv_first.shape, conv_first.dtype),
            pltpu.VMEM(conv_second.shape, conv_second.dtype),
            own,
            edge,
            own,
            edge,
            ext,
            ext,
            pltpu.VMEM((frames, height, 3 * chan, width), jnp.float32),
            pltpu.VMEM((frames, height, chan, width), jnp.float32),
            pltpu.SemaphoreType.DMA((8,)),
            pltpu.SemaphoreType.DMA((40,)),
            pltpu.SemaphoreType.DMA((40,)),
        ],
        compiler_params=pltpu.CompilerParams(
            collective_id=0, has_side_effects=True, vmem_limit_bytes=32 << 20
        ),
        cost_estimate=pl.CostEstimate(
            flops=4 * 27 * chan * chan * frames * height * width,
            bytes_accessed=3 << 20,
            transcendentals=0,
        ),
        name="residual_block",
    )(*operands)


def solution(mesh):
    placed = (P("tm", None, "rows", None), P(), P(), P(), P())
    return jax.shard_map(
        functools.partial(on_device, mesh.shape["tm"], mesh.shape["rows"]),
        mesh=mesh,
        in_specs=placed,
        out_specs=P("tm", None, "rows", None),
        check_vma=False,
    )
```

```python
import functools

import jax
import jax.numpy as jnp
from jax import lax
from jax.experimental import pallas as pl
from jax.experimental.pallas import tpu as pltpu
from jax.sharding import PartitionSpec as P

MESH = pl.DeviceIdType.MESH
epsilon = 1e-06


def norm_silu(values, gain):
    mean_square = jnp.mean(values * values, axis=0, keepdims=True)
    v = values * lax.rsqrt(mean_square + epsilon) * gain
    return (v / (1.0 + jnp.exp(-v))).astype(jnp.bfloat16)


def stack_taps(taps, own, edge):
    chan = taps.shape[-1]
    depth = own.shape[-1]
    for row, (inside, beyond) in enumerate((((1, 2), 0), ((0, 1), 2))):
        for e in range(3):
            span = slice(chan * e, chan * (e + 1))
            wide = jnp.concatenate(
                [taps[a, b, e] for a in range(3) for b in inside]
                + [taps[a, beyond, e] for a in range(3)],
                axis=1,
            )
            own[row, span, :] = wide[:, :depth]
            edge[row, span, :] = wide[:, depth:]


def as_column(row):
    chan = row.shape[0]
    wide = jnp.broadcast_to(row[None, :], (chan, chan))
    i = lax.broadcasted_iota(jnp.int32, (chan, chan), 0)
    j = lax.broadcasted_iota(jnp.int32, (chan, chan), 1)
    return jnp.sum(jnp.where(i == j, wide, 0.0), axis=1, keepdims=True)


def from_own(cells, stacked, frame, row):
    chan, width = cells.shape[2], cells.shape[3]
    window = [
        cells[frame - 2, 1:3].reshape(2 * chan, width),
        cells[frame - 1, 1:3].reshape(2 * chan, width),
        cells[frame, 1],
        cells[frame, 2, : stacked.shape[-1] - 5 * chan],
    ]
    return jnp.dot(
        stacked[row], jnp.concatenate(window, axis=0), preferred_element_type=jnp.float32
    )


def from_edge(cells, stacked, frame, row):
    chan = cells.shape[2]
    window = [cells[frame, 2, 4 * chan - stacked.shape[-1] :]]
    window += [cells[frame - 2 + a, 3 * row] for a in range(3)]
    return jnp.dot(
        stacked[row], jnp.concatenate(window, axis=0), preferred_element_type=jnp.float32
    )


def gather_columns(p):
    chan, width = p.shape[0] // 3, p.shape[1]
    column = lax.broadcasted_iota(jnp.int32, (chan, width), 1)
    before = jnp.where(column == 0, 0.0, pltpu.roll(p[:chan], 1, 1))
    after = jnp.where(
        column == width - 1, 0.0, pltpu.roll(p[2 * chan :], width - 1, 1)
    )
    return before + p[chan : 2 * chan] + after


def kernel(
    tm, rows, feat_hbm, gain1_hbm, taps1_hbm, gain2_hbm, taps2_hbm, out,
    feat, gain1, gain2, taps1, taps2, own1, edge1, own2, edge2, ext1, ext2, part, mixed,
    load_sem, send_sem, recv_sem,
):
    t = lax.axis_index("tm")
    r = lax.axis_index("rows")
    core = lax.rem(r, 2)
    chan, width = feat.shape[1], feat.shape[3]
    last = feat.shape[0] + 2

    outer_at = r - 1 + 2 * core
    has_outer = jnp.logical_and(outer_at >= 0, outer_at < rows)
    outer = (t, jnp.clip(outer_at, 0, rows - 1))
    inner = (t, r + 1 - 2 * core)
    has_next = t < tm - 1
    has_prev = t > 0
    after = (jnp.minimum(t + 1, tm - 1), r)
    before = (jnp.maximum(t - 1, 0), r)
    own_outer, own_inner = 1 + core, 2 - core
    to_outer, to_inner = 3 - 3 * core, 3 * core

    barrier = pltpu.get_barrier_semaphore()
    pl.semaphore_signal(barrier, inc=1, device_id=inner, device_id_type=MESH)

    @pl.when(has_outer)
    def _():
        pl.semaphore_signal(barrier, inc=1, device_id=outer, device_id_type=MESH)

    @pl.when(has_prev)
    def _():
        pl.semaphore_signal(barrier, inc=1, device_id=before, device_id_type=MESH)

    order = (3, 2, 1, 0)
    feat_in = {
        f: pltpu.make_async_copy(feat_hbm.at[f], feat.at[f], load_sem.at[f])
        for f in order
    }
    rest_in = [
        pltpu.make_async_copy(src, dst, load_sem.at[4 + i])
        for i, (src, dst) in enumerate(
            ((gain1_hbm, gain1), (gain2_hbm, gain2), (taps1_hbm, taps1), (taps2_hbm, taps2))
        )
    ]
    rest_in[0].start()
    for f in order:
        feat_in[f].start()
    for copy in rest_in[1:]:
        copy.start()

    def remote(ext, n, src_frames, src_row, dst_frames, dst_row, device):
        return pltpu.make_async_remote_copy(
            src_ref=ext.at[src_frames, src_row],
            dst_ref=ext.at[dst_frames, dst_row],
            send_sem=send_sem.at[n],
            recv_sem=recv_sem.at[n],
            device_id=device,
            device_id_type=MESH,
        )

    both = jnp.logical_and(has_prev, has_outer)
    moves = {}

    def plan_z(name, ext, row, cuts):
        for i, (low, high) in enumerate(cuts):
            moves[name, i] = (
                remote(ext, len(moves), slice(low + 4, high + 4), row, slice(low, high), row, after),
                has_next,
                has_prev,
            )

    def plan_rows(name, ext, cuts, relayed=False):
        for i, (low, high) in enumerate(cuts):
            frames = slice(low, high)
            condition = both if relayed else has_outer
            moves[name + "_outer", i] = (
                remote(ext, len(moves), frames, own_outer, frames, to_outer, outer),
                condition,
                condition,
            )
            condition = has_prev if relayed else None
            moves[name + "_inner", i] = (
                remote(ext, len(moves), frames, own_inner, frames, to_inner, inner),
                condition,
                condition,
            )

    halves = ((0, 1), (1, 2))
    plan_z("z1_outer", ext1, own_outer, halves)
    plan_z("z1_inner", ext1, own_inner, ((0, 2),))
    plan_rows("rows1", ext1, ((2, 3), (3, 4), (4, 5), (5, 6)))
    plan_rows("relay1", ext1, halves, True)
    plan_z("z2_outer", ext2, own_outer, halves)
    plan_z("z2_inner", ext2, own_inner, halves)
    plan_rows("late2", ext2, ((4, 6),))
    plan_rows("early2", ext2, ((2, 3), (3, 4)))
    plan_rows("relay2", ext2, halves, True)

    def when(condition, action):
        if condition is None:
            action()
        else:
            pl.when(condition)(action)

    def send(name, i=0):
        copy, sends, _ = moves[name, i]
        when(sends, copy.start)

    def got(name, i=0):
        copy, _, gets = moves[name, i]
        when(gets, copy.wait_recv)

    zero_row = jnp.zeros((chan, width), jnp.bfloat16)

    @pl.when(t == 0)
    def _():
        for ext in (ext1, ext2):
            for f in range(2):
                for row in range(4):
                    ext[f, row] = zero_row

    @pl.when(jnp.logical_not(has_outer))
    def _():
        for ext in (ext1, ext2):
            for f in range(last):
                ext[f, 3 * core] = zero_row

    rest_in[0].wait()
    column1 = as_column(gain1[...])

    def first(f):
        feat_in[f].wait()
        x = feat[f].astype(jnp.float32).reshape(chan, 2 * width)
        for row in range(2):
            ext1[2 + f, 1 + row] = norm_silu(x[:, row * width : (row + 1) * width], column1)

    neighbours = 1 + has_outer.astype(jnp.int32) + has_next.astype(jnp.int32)
    for f in order:
        first(f)
        if f == 3:
            pl.semaphore_wait(barrier, neighbours)
            send("z1_outer", 1)
        send("rows1_outer", f)
        send("rows1_inner", f)
    send("z1_outer", 0)

    out_outer, out_inner = core, 1 - core

    def start1(frame):
        for row in range(2):
            part[frame - 2, row] = from_own(ext1, own1, frame, row)

    def second(frame, row):
        p = part[frame - 2, row] + from_edge(ext1, edge1, frame, row)
        ext2[frame, 1 + row] = norm_silu(gather_columns(p), column2)

    for copy in rest_in[1:]:
        copy.wait()
    stack_taps(taps1, own1, edge1)
    column2 = as_column(gain2[...])
    start1(5)
    start1(4)
    for f in order:
        got("rows1_inner", f)
    send("z1_inner")
    second(5, out_inner)
    second(4, out_inner)
    stack_taps(taps2, own2, edge2)
    got("z1_outer", 1)
    send("relay1_outer", 1)
    send("z2_inner", 1)
    for f in order[:3]:
        got("rows1_outer", f)
    got("z1_outer", 0)
    send("relay1_outer", 0)
    got("rows1_outer", 0)
    second(5, out_outer)
    second(4, out_outer)
    send("z2_outer", 1)
    send("z2_outer", 0)
    send("late2_outer")
    send("late2_inner")
    got("z1_inner")
    for i in (1, 0):
        send("relay1_inner", i)
    send("z2_inner", 0)
    start1(3)
    start1(2)
    got("relay1_outer", 1)
    second(3, out_outer)
    send("early2_outer", 1)
    got("relay1_outer", 0)
    second(2, out_outer)
    send("early2_outer", 0)
    got("z2_inner", 1)
    send("relay2_inner", 1)
    for i in (1, 0):
        got("relay1_inner", i)
    second(3, out_inner)
    second(2, out_inner)
    for i in (1, 0):
        send("early2_inner", i)
    got("z2_outer", 1)
    send("relay2_outer", 1)

    def start2(frame):
        for row in range(2):
            part[frame - 2, row] = from_own(ext2, own2, frame, row)

    def mix(frame, row):
        p = part[frame - 2, row] + from_edge(ext2, edge2, frame, row)
        mixed[frame - 2, row] = gather_columns(p)

    def finish(frame):
        x = feat[frame - 2].astype(jnp.float32).reshape(chan, 2 * width)
        total = jnp.concatenate([mixed[frame - 2, 0], mixed[frame - 2, 1]], axis=1) + x
        out[frame - 2] = total.reshape(chan, 2, width).astype(jnp.bfloat16)

    start2(5)
    start2(4)
    got("z2_outer", 0)
    send("relay2_outer", 0)
    got("late2_inner")
    for i in (1, 0):
        got("early2_inner", i)
    mix(5, out_inner)
    mix(4, out_inner)
    start2(3)
    got("z2_inner", 0)
    send("relay2_inner", 0)
    start2(2)
    got("late2_outer")
    for i in (1, 0):
        got("early2_outer", i)
    mix(5, out_outer)
    mix(4, out_outer)
    finish(5)
    finish(4)
    got("relay2_outer", 1)
    got("relay2_inner", 1)
    mix(3, 0)
    mix(3, 1)
    finish(3)
    got("relay2_outer", 0)
    got("relay2_inner", 0)
    mix(2, 0)
    mix(2, 1)
    finish(2)

    for copy, sends, _ in moves.values():
        when(sends, copy.wait_send)


def on_device(tm, rows, features, gain_first, conv_first, gain_second, conv_second):
    frames, chan, height, width = features.shape
    ext = pltpu.VMEM((frames + 2, height + 2, chan, width), jnp.bfloat16)
    depth = 6 * chan // 256 * 256
    own = pltpu.VMEM((2, 3 * chan, depth), jnp.bfloat16)
    edge = pltpu.VMEM((2, 3 * chan, 9 * chan - depth), jnp.bfloat16)
    operands = (features, gain_first, conv_first, gain_second, conv_second)
    operands = [pltpu.with_memory_space_constraint(x, pltpu.HBM) for x in operands]
    return pl.pallas_call(
        functools.partial(kernel, tm, rows),
        out_shape=pltpu.VMEM(features.shape, features.dtype),
        in_specs=[pl.BlockSpec(memory_space=pl.ANY)] * 5,
        out_specs=pl.BlockSpec(memory_space=pltpu.VMEM),
        scratch_shapes=[
            pltpu.VMEM(features.shape, features.dtype),
            pltpu.VMEM(gain_first.shape, gain_first.dtype),
            pltpu.VMEM(gain_second.shape, gain_second.dtype),
            pltpu.VMEM(conv_first.shape, conv_first.dtype),
            pltpu.VMEM(conv_second.shape, conv_second.dtype),
            own,
            edge,
            own,
            edge,
            ext,
            ext,
            pltpu.VMEM((frames, height, 3 * chan, width), jnp.float32),
            pltpu.VMEM((frames, height, chan, width), jnp.float32),
            pltpu.SemaphoreType.DMA((8,)),
            pltpu.SemaphoreType.DMA((40,)),
            pltpu.SemaphoreType.DMA((40,)),
        ],
        compiler_params=pltpu.CompilerParams(
            collective_id=0, has_side_effects=True, vmem_limit_bytes=32 << 20
        ),
        cost_estimate=pl.CostEstimate(
            flops=4 * 27 * chan * chan * frames * height * width,
            bytes_accessed=3 << 20,
            transcendentals=0,
        ),
        name="residual_block",
    )(*operands)


def solution(mesh):
    placed = (P("tm", None, "rows", None), P(), P(), P(), P())
    return jax.shard_map(
        functools.partial(on_device, mesh.shape["tm"], mesh.shape["rows"]),
        mesh=mesh,
        in_specs=placed,
        out_specs=P("tm", None, "rows", None),
        check_vma=False,
    )
```

```python
import functools

import jax
import jax.numpy as jnp
from jax import lax
from jax.experimental import pallas as pl
from jax.experimental.pallas import tpu as pltpu
from jax.sharding import PartitionSpec as P

MESH = pl.DeviceIdType.MESH
epsilon = 1e-06


def norm_silu(values, gain):
    mean_square = jnp.mean(values * values, axis=0, keepdims=True)
    v = values * lax.rsqrt(mean_square + epsilon) * gain
    return (v / (1.0 + jnp.exp(-v))).astype(jnp.bfloat16)


def stack_taps(taps, own, edge):
    chan = taps.shape[-1]
    depth = own.shape[-1]
    for row, (inside, beyond) in enumerate((((1, 2), 0), ((0, 1), 2))):
        for e in range(3):
            span = slice(chan * e, chan * (e + 1))
            wide = jnp.concatenate(
                [taps[a, b, e] for a in range(3) for b in inside]
                + [taps[a, beyond, e] for a in range(3)],
                axis=1,
            )
            own[row, span, :] = wide[:, :depth]
            edge[row, span, :] = wide[:, depth:]


def as_column(row):
    chan = row.shape[0]
    wide = jnp.broadcast_to(row[None, :], (chan, chan))
    i = lax.broadcasted_iota(jnp.int32, (chan, chan), 0)
    j = lax.broadcasted_iota(jnp.int32, (chan, chan), 1)
    return jnp.sum(jnp.where(i == j, wide, 0.0), axis=1, keepdims=True)


def from_own(cells, stacked, frame, row):
    chan, width = cells.shape[2], cells.shape[3]
    window = [
        cells[frame - 2, 1:3].reshape(2 * chan, width),
        cells[frame - 1, 1:3].reshape(2 * chan, width),
        cells[frame, 1],
        cells[frame, 2, : stacked.shape[-1] - 5 * chan],
    ]
    return jnp.dot(
        stacked[row], jnp.concatenate(window, axis=0), preferred_element_type=jnp.float32
    )


def from_edge(cells, stacked, frame, row):
    chan = cells.shape[2]
    window = [cells[frame, 2, 4 * chan - stacked.shape[-1] :]]
    window += [cells[frame - 2 + a, 3 * row] for a in range(3)]
    return jnp.dot(
        stacked[row], jnp.concatenate(window, axis=0), preferred_element_type=jnp.float32
    )


def gather_columns(p):
    chan, width = p.shape[0] // 3, p.shape[1]
    column = lax.broadcasted_iota(jnp.int32, (chan, width), 1)
    before = jnp.where(column == 0, 0.0, pltpu.roll(p[:chan], 1, 1))
    after = jnp.where(
        column == width - 1, 0.0, pltpu.roll(p[2 * chan :], width - 1, 1)
    )
    return before + p[chan : 2 * chan] + after


def kernel(
    tm, rows, feat_hbm, gain1_hbm, taps1_hbm, gain2_hbm, taps2_hbm, out,
    feat, gain1, gain2, taps1, taps2, own1, edge1, own2, edge2, ext1, ext2, part, mixed,
    load_sem, send_sem, recv_sem,
):
    t = lax.axis_index("tm")
    r = lax.axis_index("rows")
    core = lax.rem(r, 2)
    chan, width = feat.shape[1], feat.shape[3]
    last = feat.shape[0] + 2

    outer_at = r - 1 + 2 * core
    has_outer = jnp.logical_and(outer_at >= 0, outer_at < rows)
    outer = (t, jnp.clip(outer_at, 0, rows - 1))
    inner = (t, r + 1 - 2 * core)
    has_next = t < tm - 1
    has_prev = t > 0
    after = (jnp.minimum(t + 1, tm - 1), r)
    before = (jnp.maximum(t - 1, 0), r)
    own_outer, own_inner = 1 + core, 2 - core
    to_outer, to_inner = 3 - 3 * core, 3 * core

    barrier = pltpu.get_barrier_semaphore()
    pl.semaphore_signal(barrier, inc=1, device_id=inner, device_id_type=MESH)

    @pl.when(has_outer)
    def _():
        pl.semaphore_signal(barrier, inc=1, device_id=outer, device_id_type=MESH)

    @pl.when(has_prev)
    def _():
        pl.semaphore_signal(barrier, inc=1, device_id=before, device_id_type=MESH)

    order = (3, 2, 1, 0)
    feat_in = {
        f: pltpu.make_async_copy(feat_hbm.at[f], feat.at[f], load_sem.at[f])
        for f in order
    }
    rest_in = [
        pltpu.make_async_copy(src, dst, load_sem.at[4 + i])
        for i, (src, dst) in enumerate(
            ((gain1_hbm, gain1), (gain2_hbm, gain2), (taps1_hbm, taps1), (taps2_hbm, taps2))
        )
    ]
    rest_in[0].start()
    for f in order:
        feat_in[f].start()
    for copy in rest_in[1:]:
        copy.start()

    def remote(ext, n, src_frames, src_row, dst_frames, dst_row, device):
        return pltpu.make_async_remote_copy(
            src_ref=ext.at[src_frames, src_row],
            dst_ref=ext.at[dst_frames, dst_row],
            send_sem=send_sem.at[n],
            recv_sem=recv_sem.at[n],
            device_id=device,
            device_id_type=MESH,
        )

    both = jnp.logical_and(has_prev, has_outer)
    moves = {}

    def plan_z(name, ext, row, cuts):
        for i, (low, high) in enumerate(cuts):
            moves[name, i] = (
                remote(ext, len(moves), slice(low + 4, high + 4), row, slice(low, high), row, after),
                has_next,
                has_prev,
            )

    def plan_rows(name, ext, cuts, relayed=False):
        for i, (low, high) in enumerate(cuts):
            frames = slice(low, high)
            condition = both if relayed else has_outer
            moves[name + "_outer", i] = (
                remote(ext, len(moves), frames, own_outer, frames, to_outer, outer),
                condition,
                condition,
            )
            condition = has_prev if relayed else None
            moves[name + "_inner", i] = (
                remote(ext, len(moves), frames, own_inner, frames, to_inner, inner),
                condition,
                condition,
            )

    halves = ((0, 1), (1, 2))
    plan_z("z1_outer", ext1, own_outer, halves)
    plan_z("z1_inner", ext1, own_inner, ((0, 2),))
    plan_rows("rows1", ext1, ((2, 3), (3, 4), (4, 5), (5, 6)))
    plan_rows("relay1", ext1, halves, True)
    plan_z("z2_outer", ext2, own_outer, halves)
    plan_z("z2_inner", ext2, own_inner, halves)
    plan_rows("late2", ext2, ((4, 6),))
    plan_rows("early2", ext2, ((2, 3), (3, 4)))
    plan_rows("relay2", ext2, halves, True)

    def when(condition, action):
        if condition is None:
            action()
        else:
            pl.when(condition)(action)

    def send(name, i=0):
        copy, sends, _ = moves[name, i]
        when(sends, copy.start)

    def got(name, i=0):
        copy, _, gets = moves[name, i]
        when(gets, copy.wait_recv)

    def sent(*names):
        for (name, _), (copy, sends, _) in moves.items():
            if name in names:
                when(sends, copy.wait_send)

    zero_row = jnp.zeros((chan, width), jnp.bfloat16)

    @pl.when(t == 0)
    def _():
        for ext in (ext1, ext2):
            for f in range(2):
                for row in range(4):
                    ext[f, row] = zero_row

    @pl.when(jnp.logical_not(has_outer))
    def _():
        for ext in (ext1, ext2):
            for f in range(last):
                ext[f, 3 * core] = zero_row

    rest_in[0].wait()
    column1 = as_column(gain1[...])

    def first(f):
        feat_in[f].wait()
        x = feat[f].astype(jnp.float32).reshape(chan, 2 * width)
        for row in range(2):
            ext1[2 + f, 1 + row] = norm_silu(x[:, row * width : (row + 1) * width], column1)

    neighbours = 1 + has_outer.astype(jnp.int32) + has_next.astype(jnp.int32)
    for f in order:
        first(f)
        if f == 3:
            pl.semaphore_wait(barrier, neighbours)
            send("z1_outer", 1)
        send("rows1_outer", f)
        send("rows1_inner", f)
    send("z1_outer", 0)

    below = t == tm // 2 - 1

    def pass_on(i):
        got("z1_outer", i)
        send("relay1_outer", i)

    @pl.when(below)
    def _():
        pass_on(1)
        pass_on(0)

    out_outer, out_inner = core, 1 - core

    def start1(frame):
        for row in range(2):
            part[frame - 2, row] = from_own(ext1, own1, frame, row)

    def second(frame, row):
        p = part[frame - 2, row] + from_edge(ext1, edge1, frame, row)
        ext2[frame, 1 + row] = norm_silu(gather_columns(p), column2)

    for copy in rest_in[1:]:
        copy.wait()
    stack_taps(taps1, own1, edge1)
    column2 = as_column(gain2[...])
    start1(5)
    start1(4)
    for f in order:
        got("rows1_inner", f)
    send("z1_inner")
    second(5, out_inner)
    second(4, out_inner)
    stack_taps(taps2, own2, edge2)
    pl.when(jnp.logical_not(below))(functools.partial(pass_on, 1))
    send("z2_inner", 1)
    for f in order[:3]:
        got("rows1_outer", f)
    pl.when(jnp.logical_not(below))(functools.partial(pass_on, 0))
    got("rows1_outer", 0)
    second(5, out_outer)
    second(4, out_outer)
    send("z2_outer", 1)
    send("z2_outer", 0)
    send("late2_outer")
    send("late2_inner")
    got("z1_inner")
    for i in (1, 0):
        send("relay1_inner", i)
    send("z2_inner", 0)
    start1(3)
    start1(2)
    got("relay1_outer", 1)
    second(3, out_outer)
    send("early2_outer", 1)
    got("relay1_outer", 0)
    second(2, out_outer)
    send("early2_outer", 0)
    got("z2_inner", 1)
    send("relay2_inner", 1)
    for i in (1, 0):
        got("relay1_inner", i)
    second(3, out_inner)
    second(2, out_inner)
    for i in (1, 0):
        send("early2_inner", i)
    got("z2_outer", 1)
    send("relay2_outer", 1)

    def start2(frame):
        for row in range(2):
            part[frame - 2, row] = from_own(ext2, own2, frame, row)

    def mix(frame, row):
        p = part[frame - 2, row] + from_edge(ext2, edge2, frame, row)
        mixed[frame - 2, row] = gather_columns(p)

    def finish(frame):
        x = feat[frame - 2].astype(jnp.float32).reshape(chan, 2 * width)
        total = jnp.concatenate([mixed[frame - 2, 0], mixed[frame - 2, 1]], axis=1) + x
        out[frame - 2] = total.reshape(chan, 2, width).astype(jnp.bfloat16)

    start2(5)
    start2(4)
    got("z2_outer", 0)
    send("relay2_outer", 0)
    got("late2_inner")
    for i in (1, 0):
        got("early2_inner", i)
    mix(5, out_inner)
    mix(4, out_inner)
    start2(3)
    got("z2_inner", 0)
    send("relay2_inner", 0)
    start2(2)
    got("late2_outer")
    for i in (1, 0):
        got("early2_outer", i)
    mix(5, out_outer)
    mix(4, out_outer)
    finish(5)
    finish(4)
    sent(*({name for name, _ in moves} - {"relay2_outer", "relay2_inner"}))
    got("relay2_outer", 1)
    got("relay2_inner", 1)
    mix(3, 0)
    mix(3, 1)
    finish(3)
    got("relay2_outer", 0)
    got("relay2_inner", 0)
    mix(2, 0)
    mix(2, 1)
    finish(2)

    sent("relay2_outer", "relay2_inner")


def on_device(tm, rows, features, gain_first, conv_first, gain_second, conv_second):
    frames, chan, height, width = features.shape
    ext = pltpu.VMEM((frames + 2, height + 2, chan, width), jnp.bfloat16)
    depth = 6 * chan // 256 * 256
    own = pltpu.VMEM((2, 3 * chan, depth), jnp.bfloat16)
    edge = pltpu.VMEM((2, 3 * chan, 9 * chan - depth), jnp.bfloat16)
    operands = (features, gain_first, conv_first, gain_second, conv_second)
    operands = [pltpu.with_memory_space_constraint(x, pltpu.HBM) for x in operands]
    return pl.pallas_call(
        functools.partial(kernel, tm, rows),
        out_shape=pltpu.VMEM(features.shape, features.dtype),
        in_specs=[pl.BlockSpec(memory_space=pl.ANY)] * 5,
        out_specs=pl.BlockSpec(memory_space=pltpu.VMEM),
        scratch_shapes=[
            pltpu.VMEM(features.shape, features.dtype),
            pltpu.VMEM(gain_first.shape, gain_first.dtype),
            pltpu.VMEM(gain_second.shape, gain_second.dtype),
            pltpu.VMEM(conv_first.shape, conv_first.dtype),
            pltpu.VMEM(conv_second.shape, conv_second.dtype),
            own,
            edge,
            own,
            edge,
            ext,
            ext,
            pltpu.VMEM((frames, height, 3 * chan, width), jnp.float32),
            pltpu.VMEM((frames, height, chan, width), jnp.float32),
            pltpu.SemaphoreType.DMA((8,)),
            pltpu.SemaphoreType.DMA((40,)),
            pltpu.SemaphoreType.DMA((40,)),
        ],
        compiler_params=pltpu.CompilerParams(
            collective_id=0, has_side_effects=True, vmem_limit_bytes=32 << 20
        ),
        cost_estimate=pl.CostEstimate(
            flops=4 * 27 * chan * chan * frames * height * width,
            bytes_accessed=3 << 20,
            transcendentals=0,
        ),
        name="residual_block",
    )(*operands)


def solution(mesh):
    placed = (P("tm", None, "rows", None), P(), P(), P(), P())
    return jax.shard_map(
        functools.partial(on_device, mesh.shape["tm"], mesh.shape["rows"]),
        mesh=mesh,
        in_specs=placed,
        out_specs=P("tm", None, "rows", None),
        check_vma=False,
    )
```

```python
import functools

import jax
import jax.numpy as jnp
from jax import lax
from jax.experimental import pallas as pl
from jax.experimental.pallas import tpu as pltpu
from jax.sharding import PartitionSpec as P

MESH = pl.DeviceIdType.MESH
epsilon = 1e-06


def norm_silu(values, gain):
    mean_square = jnp.mean(values * values, axis=0, keepdims=True)
    v = values * lax.rsqrt(mean_square + epsilon) * gain
    half = 0.5 * v
    return (half + half * jnp.tanh(half)).astype(jnp.bfloat16)


def stack_taps(taps, own, edge):
    chan = taps.shape[-1]
    depth = own.shape[-1]
    for row, (inside, beyond) in enumerate((((1, 2), 0), ((0, 1), 2))):
        for e in range(3):
            span = slice(chan * e, chan * (e + 1))
            wide = jnp.concatenate(
                [taps[a, b, e] for a in range(3) for b in inside]
                + [taps[a, beyond, e] for a in range(3)],
                axis=1,
            )
            own[row, span, :] = wide[:, :depth]
            edge[row, span, :] = wide[:, depth:]


def as_column(row):
    chan = row.shape[0]
    wide = jnp.broadcast_to(row[None, :], (chan, chan))
    i = lax.broadcasted_iota(jnp.int32, (chan, chan), 0)
    j = lax.broadcasted_iota(jnp.int32, (chan, chan), 1)
    return jnp.sum(jnp.where(i == j, wide, 0.0), axis=1, keepdims=True)


def from_own(cells, stacked, frame, row):
    chan, width = cells.shape[2], cells.shape[3]
    window = [
        cells[frame - 2, 1:3].reshape(2 * chan, width),
        cells[frame - 1, 1:3].reshape(2 * chan, width),
        cells[frame, 1],
        cells[frame, 2, : stacked.shape[-1] - 5 * chan],
    ]
    return jnp.dot(
        stacked[row], jnp.concatenate(window, axis=0), preferred_element_type=jnp.float32
    )


def from_edge(cells, stacked, frame, row):
    chan = cells.shape[2]
    window = [cells[frame, 2, 4 * chan - stacked.shape[-1] :]]
    window += [cells[frame - 2 + a, 3 * row] for a in range(3)]
    return jnp.dot(
        stacked[row], jnp.concatenate(window, axis=0), preferred_element_type=jnp.float32
    )


def gather_columns(p):
    chan, width = p.shape[0] // 3, p.shape[1]
    column = lax.broadcasted_iota(jnp.int32, (chan, width), 1)
    before = jnp.where(column == 0, 0.0, pltpu.roll(p[:chan], 1, 1))
    after = jnp.where(
        column == width - 1, 0.0, pltpu.roll(p[2 * chan :], width - 1, 1)
    )
    return before + p[chan : 2 * chan] + after


def kernel(
    tm, rows, feat_hbm, gain1_hbm, taps1_hbm, gain2_hbm, taps2_hbm, out,
    feat, gain1, gain2, taps1, taps2, own1, edge1, own2, edge2, ext1, ext2, part, mixed,
    load_sem, send_sem, recv_sem,
):
    t = lax.axis_index("tm")
    r = lax.axis_index("rows")
    core = lax.rem(r, 2)
    chan, width = feat.shape[1], feat.shape[3]
    last = feat.shape[0] + 2

    outer_at = r - 1 + 2 * core
    has_outer = jnp.logical_and(outer_at >= 0, outer_at < rows)
    outer = (t, jnp.clip(outer_at, 0, rows - 1))
    inner = (t, r + 1 - 2 * core)
    has_next = t < tm - 1
    has_prev = t > 0
    after = (jnp.minimum(t + 1, tm - 1), r)
    before = (jnp.maximum(t - 1, 0), r)
    own_outer, own_inner = 1 + core, 2 - core
    to_outer, to_inner = 3 - 3 * core, 3 * core

    barrier = pltpu.get_barrier_semaphore()
    pl.semaphore_signal(barrier, inc=1, device_id=inner, device_id_type=MESH)

    @pl.when(has_outer)
    def _():
        pl.semaphore_signal(barrier, inc=1, device_id=outer, device_id_type=MESH)

    @pl.when(has_prev)
    def _():
        pl.semaphore_signal(barrier, inc=1, device_id=before, device_id_type=MESH)

    order = (3, 2, 1, 0)
    feat_in = {
        f: pltpu.make_async_copy(feat_hbm.at[f], feat.at[f], load_sem.at[f])
        for f in order
    }
    rest_in = [
        pltpu.make_async_copy(src, dst, load_sem.at[4 + i])
        for i, (src, dst) in enumerate(
            ((gain1_hbm, gain1), (gain2_hbm, gain2), (taps1_hbm, taps1), (taps2_hbm, taps2))
        )
    ]
    rest_in[0].start()
    for f in order:
        feat_in[f].start()
    for copy in rest_in[1:]:
        copy.start()

    def remote(ext, n, src_frames, src_row, dst_frames, dst_row, device):
        return pltpu.make_async_remote_copy(
            src_ref=ext.at[src_frames, src_row],
            dst_ref=ext.at[dst_frames, dst_row],
            send_sem=send_sem.at[n],
            recv_sem=recv_sem.at[n],
            device_id=device,
            device_id_type=MESH,
        )

    both = jnp.logical_and(has_prev, has_outer)
    moves = {}

    def plan_z(name, ext, row, cuts):
        for i, (low, high) in enumerate(cuts):
            moves[name, i] = (
                remote(ext, len(moves), slice(low + 4, high + 4), row, slice(low, high), row, after),
                has_next,
                has_prev,
            )

    def plan_rows(name, ext, cuts, relayed=False):
        for i, (low, high) in enumerate(cuts):
            frames = slice(low, high)
            condition = both if relayed else has_outer
            moves[name + "_outer", i] = (
                remote(ext, len(moves), frames, own_outer, frames, to_outer, outer),
                condition,
                condition,
            )
            condition = has_prev if relayed else None
            moves[name + "_inner", i] = (
                remote(ext, len(moves), frames, own_inner, frames, to_inner, inner),
                condition,
                condition,
            )

    halves = ((0, 1), (1, 2))
    plan_z("z1_outer", ext1, own_outer, halves)
    plan_z("z1_inner", ext1, own_inner, ((0, 2),))
    plan_rows("rows1", ext1, ((2, 3), (3, 4), (4, 5), (5, 6)))
    plan_rows("relay1", ext1, halves, True)
    plan_z("z2_outer", ext2, own_outer, halves)
    plan_z("z2_inner", ext2, own_inner, halves)
    plan_rows("late2", ext2, ((4, 6),))
    plan_rows("early2", ext2, ((2, 3), (3, 4)))
    plan_rows("relay2", ext2, halves, True)

    def when(condition, action):
        if condition is None:
            action()
        else:
            pl.when(condition)(action)

    def send(name, i=0):
        copy, sends, _ = moves[name, i]
        when(sends, copy.start)

    def got(name, i=0):
        copy, _, gets = moves[name, i]
        when(gets, copy.wait_recv)

    def sent(*names):
        for (name, _), (copy, sends, _) in moves.items():
            if name in names:
                when(sends, copy.wait_send)

    zero_row = jnp.zeros((chan, width), jnp.bfloat16)

    @pl.when(t == 0)
    def _():
        for ext in (ext1, ext2):
            for f in range(2):
                for row in range(4):
                    ext[f, row] = zero_row

    @pl.when(jnp.logical_not(has_outer))
    def _():
        for ext in (ext1, ext2):
            for f in range(last):
                ext[f, 3 * core] = zero_row

    rest_in[0].wait()
    column1 = as_column(gain1[...])

    def first(f):
        feat_in[f].wait()
        x = feat[f].astype(jnp.float32).reshape(chan, 2 * width)
        for row in range(2):
            ext1[2 + f, 1 + row] = norm_silu(x[:, row * width : (row + 1) * width], column1)

    neighbours = 1 + has_outer.astype(jnp.int32) + has_next.astype(jnp.int32)
    for f in order:
        first(f)
        if f == 3:
            pl.semaphore_wait(barrier, neighbours)
            send("z1_outer", 1)
        send("rows1_outer", f)
        send("rows1_inner", f)
    send("z1_outer", 0)

    below = t == tm // 2 - 1

    def pass_on(i):
        got("z1_outer", i)
        send("relay1_outer", i)

    @pl.when(below)
    def _():
        pass_on(1)
        pass_on(0)

    out_outer, out_inner = core, 1 - core

    def start1(frame):
        for row in range(2):
            part[frame - 2, row] = from_own(ext1, own1, frame, row)

    def second(frame, row):
        p = part[frame - 2, row] + from_edge(ext1, edge1, frame, row)
        ext2[frame, 1 + row] = norm_silu(gather_columns(p), column2)

    for copy in rest_in[1:]:
        copy.wait()
    stack_taps(taps1, own1, edge1)
    column2 = as_column(gain2[...])
    start1(5)
    start1(4)
    for f in order:
        got("rows1_inner", f)
    send("z1_inner")
    second(5, out_inner)
    second(4, out_inner)
    stack_taps(taps2, own2, edge2)
    pl.when(jnp.logical_not(below))(functools.partial(pass_on, 1))
    send("z2_inner", 1)
    for f in order[:3]:
        got("rows1_outer", f)
    pl.when(jnp.logical_not(below))(functools.partial(pass_on, 0))
    got("rows1_outer", 0)
    second(5, out_outer)
    second(4, out_outer)
    send("z2_outer", 1)
    send("z2_outer", 0)
    send("late2_outer")
    send("late2_inner")
    got("z1_inner")
    for i in (1, 0):
        send("relay1_inner", i)
    send("z2_inner", 0)
    start1(3)
    start1(2)
    got("relay1_outer", 1)
    second(3, out_outer)
    send("early2_outer", 1)
    got("relay1_outer", 0)
    second(2, out_outer)
    send("early2_outer", 0)
    got("z2_inner", 1)
    send("relay2_inner", 1)
    for i in (1, 0):
        got("relay1_inner", i)
    second(3, out_inner)
    second(2, out_inner)
    for i in (1, 0):
        send("early2_inner", i)
    got("z2_outer", 1)
    send("relay2_outer", 1)

    def start2(frame):
        for row in range(2):
            part[frame - 2, row] = from_own(ext2, own2, frame, row)

    def mix(frame, row):
        p = part[frame - 2, row] + from_edge(ext2, edge2, frame, row)
        mixed[frame - 2, row] = gather_columns(p)

    def finish(frame):
        x = feat[frame - 2].astype(jnp.float32).reshape(chan, 2 * width)
        total = jnp.concatenate([mixed[frame - 2, 0], mixed[frame - 2, 1]], axis=1) + x
        out[frame - 2] = total.reshape(chan, 2, width).astype(jnp.bfloat16)

    start2(5)
    start2(4)
    got("z2_outer", 0)
    send("relay2_outer", 0)
    got("late2_inner")
    for i in (1, 0):
        got("early2_inner", i)
    mix(5, out_inner)
    mix(4, out_inner)
    start2(3)
    got("z2_inner", 0)
    send("relay2_inner", 0)
    start2(2)
    got("late2_outer")
    for i in (1, 0):
        got("early2_outer", i)
    mix(5, out_outer)
    mix(4, out_outer)
    finish(5)
    finish(4)
    sent(*({name for name, _ in moves} - {"relay2_outer", "relay2_inner"}))
    got("relay2_outer", 1)
    got("relay2_inner", 1)
    mix(3, 0)
    mix(3, 1)
    finish(3)
    got("relay2_outer", 0)
    got("relay2_inner", 0)
    mix(2, 0)
    mix(2, 1)
    finish(2)

    sent("relay2_outer", "relay2_inner")


def on_device(tm, rows, features, gain_first, conv_first, gain_second, conv_second):
    frames, chan, height, width = features.shape
    ext = pltpu.VMEM((frames + 2, height + 2, chan, width), jnp.bfloat16)
    depth = 6 * chan // 256 * 256
    own = pltpu.VMEM((2, 3 * chan, depth), jnp.bfloat16)
    edge = pltpu.VMEM((2, 3 * chan, 9 * chan - depth), jnp.bfloat16)
    operands = (features, gain_first, conv_first, gain_second, conv_second)
    operands = [pltpu.with_memory_space_constraint(x, pltpu.HBM) for x in operands]
    return pl.pallas_call(
        functools.partial(kernel, tm, rows),
        out_shape=pltpu.VMEM(features.shape, features.dtype),
        in_specs=[pl.BlockSpec(memory_space=pl.ANY)] * 5,
        out_specs=pl.BlockSpec(memory_space=pltpu.VMEM),
        scratch_shapes=[
            pltpu.VMEM(features.shape, features.dtype),
            pltpu.VMEM(gain_first.shape, gain_first.dtype),
            pltpu.VMEM(gain_second.shape, gain_second.dtype),
            pltpu.VMEM(conv_first.shape, conv_first.dtype),
            pltpu.VMEM(conv_second.shape, conv_second.dtype),
            own,
            edge,
            own,
            edge,
            ext,
            ext,
            pltpu.VMEM((frames, height, 3 * chan, width), jnp.float32),
            pltpu.VMEM((frames, height, chan, width), jnp.float32),
            pltpu.SemaphoreType.DMA((8,)),
            pltpu.SemaphoreType.DMA((40,)),
            pltpu.SemaphoreType.DMA((40,)),
        ],
        compiler_params=pltpu.CompilerParams(
            collective_id=0, has_side_effects=True, vmem_limit_bytes=32 << 20
        ),
        cost_estimate=pl.CostEstimate(
            flops=4 * 27 * chan * chan * frames * height * width,
            bytes_accessed=3 << 20,
            transcendentals=0,
        ),
        name="residual_block",
    )(*operands)


def solution(mesh):
    placed = (P("tm", None, "rows", None), P(), P(), P(), P())
    return jax.shard_map(
        functools.partial(on_device, mesh.shape["tm"], mesh.shape["rows"]),
        mesh=mesh,
        in_specs=placed,
        out_specs=P("tm", None, "rows", None),
        check_vma=False,
    )
```
